256 devices in a mesh: ka: 8 (over z), band: 8 (over x_lo, y), fit: 4 (over x_hi, core).
Axes of the slice: x: 4 (x_hi: 2, x_lo: 2; x = x_hi * 2 + x_lo), y: 4, z: 8, core: 2. Of those that a mesh axis runs over, the one named last changes fastest.
Arguments:
- fitted: bfloat16 [8, 2, 2048, 24576], P('ka', None, 'fit', 'band'), may hold values from -6 to 6
- omega: float32 [6, 2048], P(None, 'fit'), may hold values from 0.05 to 1
- coefficients: float32 [2, 6], replicated, may hold values from 0.2 to 1
- partner: int32 [8], replicated, may hold values from 0 to 7, as said below
Outputs:
- pair_v: float32 [2, 8, 48, 48], P(None, 'ka', 'band')
- pair_x: float32 [2, 8, 48, 48], P(None, 'ka', 'band')
The draws below stay inside these ranges and needn't reach their ends.
Inputs may be any that keep to these rules, and one draw needn't show every extreme that they name: partner is a permutation that maps the 1 k-points of each aligned block b (k-points b * 1 to b + 1 - 1) onto those of block (b + t) mod (8), in some order, for one whole t with 1 <= t < 8 shared by all blocks.
All inputs are finite; a program needn't handle non-finite values.
Results may differ from the reference program's by a relative error of at most 0.0029.
Values may be sent and summed in bfloat16 or wider, within the bound.
No kernel may reach another device: no remote copies, remote signals or barrier semaphores. Data moves between devices by JAX's collectives and lax.ppermute only.
A program may use at most 192 MiB of HBM per device.

```python
import math
import jax
import jax.numpy as jnp
from jax import lax

NOCC = 48
NCABS = 512
NAUX = 2048
GTERMS = 6
K_DEV = 1
KPTS = 8


def draw_partner(key, part):
    key = jax.random.fold_in(key, 7)
    offset_key = jax.random.fold_in(key, 1)
    order_key = jax.random.fold_in(key, 2)
    blocks = KPTS // K_DEV
    offset = jax.random.randint(offset_key, (), 1, blocks)
    block_keys = jax.random.split(order_key, blocks)
    orders = jax.vmap(lambda single: jax.random.permutation(single, K_DEV))(block_keys).astype(jnp.int32)
    block_ids = jnp.arange(blocks, dtype=jnp.int32)
    target = ((block_ids + offset) % blocks).astype(jnp.int32)
    result = target[:, None] * K_DEV + orders
    return result.reshape(KPTS).astype(jnp.int32)


def block_scale(rng, shape, cuts, low, top_value):
    gain, own = 1.0, jax.random.fold_in(rng, 6)
    for axis_at, parts in cuts:
        heights = jnp.exp(jax.random.uniform(jax.random.fold_in(own, axis_at), (parts,), jnp.float32, low / len(cuts), top_value / len(cuts)))
        gain = gain * jnp.repeat(heights, shape[axis_at] // parts).reshape([-1 if axis == axis_at else 1 for axis in range(len(shape))])
    return gain


def scatter_about(stream_key, extent, width, bound, shards=(), kind=jnp.bfloat16):
    entries = width * jax.random.normal(stream_key, extent, jnp.float32)
    if shards:
        entries = entries * block_scale(stream_key, extent, shards, -0.22, 0.18)
    return jnp.clip(entries, -bound, bound).astype(kind)


def setup_inputs(seed: int = 0) -> dict:
    splits = jax.random.split(jax.random.key(seed), 5)
    fitted = scatter_about(splits[0], (KPTS, 2, NAUX, NCABS * NOCC), 1.0, 6.0, ((0, 8), (2, 4), (3, 8)))
    omega = jnp.clip(jnp.exp(math.log(1.0) - 2.9957323 * jax.random.uniform(splits[1], (GTERMS, NAUX), jnp.float32) ** block_scale(splits[1], (GTERMS, NAUX), ((1, 4),), -0.2, 0.2)), 0.05, 1.0)
    coefficients = jnp.clip(jax.random.uniform(splits[2], (2, GTERMS), jnp.float32, 0.2, 1.0), 0.2, 1.0)
    partner = draw_partner(jax.random.fold_in(splits[4], 71), 0)
    return {"fitted": fitted, "omega": omega, "coefficients": coefficients, "partner": partner}


def complex_pair(weighted, partner_rows):
    real_part = jnp.dot(weighted[0].T, partner_rows[0], preferred_element_type=jnp.float32) + jnp.dot(weighted[1].T, partner_rows[1], preferred_element_type=jnp.float32)
    imag_part = jnp.dot(weighted[1].T, partner_rows[0], preferred_element_type=jnp.float32) - jnp.dot(weighted[0].T, partner_rows[1], preferred_element_type=jnp.float32)
    return jnp.stack([real_part, imag_part])

def reference(fitted, omega, coefficients, partner):
    kernel = jnp.dot(coefficients, omega, precision=lax.Precision.HIGHEST, preferred_element_type=jnp.float32) / math.sqrt(NAUX * NCABS)

    def single_kpoint_terms(kpoint_index):
        local_rows = lax.dynamic_index_in_dim(fitted, kpoint_index, 0, keepdims=False)
        partner_rows = lax.dynamic_index_in_dim(fitted, partner[kpoint_index].astype(jnp.int32), 0, keepdims=False)
        partner_rows = partner_rows.reshape(2, NAUX * NCABS, NOCC)
        results = []
        for geminal_operator in range(2):
            scaled = (local_rows.astype(jnp.float32) * kernel[geminal_operator][None, :, None]).astype(jnp.bfloat16)
            scaled = scaled.reshape(2, NAUX * NCABS, NOCC)
            results.append(complex_pair(scaled, partner_rows))
        return jnp.stack(results)
    stacked = lax.map(single_kpoint_terms, jnp.arange(KPTS, dtype=jnp.int32))
    pair_v = jnp.transpose(stacked[:, 0], (1, 0, 2, 3))
    pair_x = jnp.transpose(stacked[:, 1], (1, 0, 2, 3))
    return (pair_v, pair_x)
```

```python
import functools
import math

import jax
import jax.numpy as jnp
import numpy as np
from jax import lax
from jax.experimental import pallas as pl
from jax.experimental.pallas import tpu as pltpu
from jax.sharding import PartitionSpec as P

NOCC = 48
NCABS = 512
NAUX = 2048
GROUP = 8
WIDTH = GROUP * NOCC


def shifted(value, axis, by):
    devices = lax.axis_size(axis)
    return lax.ppermute(value, axis, [(i, (i + by) % devices) for i in range(devices)])


def fold_matrix(owners):
    rows = NOCC // owners
    result = np.zeros((4 * WIDTH, 4 * NOCC), np.float32)
    for term in range(4):
        for band in range(GROUP):
            for i in range(NOCC):
                column = term * WIDTH + band * NOCC + i
                result[column, (i // rows) * 4 * rows + term * rows + i % rows] = 1
    return jnp.asarray(result, jnp.bfloat16)


def pair_kernel(a_ref, b_ref, w_ref, fold_ref, out_ref, scaled, total):
    step = pl.program_id(0)
    depth = a_ref.shape[1]
    for operator in range(2):
        w = w_ref[:, operator : operator + 1]
        a0 = (a_ref[0].astype(jnp.float32) * w).astype(jnp.bfloat16)
        a1 = (a_ref[1].astype(jnp.float32) * w).astype(jnp.bfloat16)
        left = slice(2 * operator * WIDTH, (2 * operator + 1) * WIDTH)
        right = slice((2 * operator + 1) * WIDTH, (2 * operator + 2) * WIDTH)
        scaled[:depth, left] = a0
        scaled[depth:, left] = a1
        scaled[:depth, right] = a1
        scaled[depth:, right] = -a0
    b = b_ref[...].reshape(2 * depth, WIDTH)
    product = lax.dot_general(
        b, scaled[...], (((0,), (0,)), ((), ())), preferred_element_type=jnp.float32
    )

    @pl.when(step == 0)
    def _():
        total[...] = product

    @pl.when(step > 0)
    def _():
        total[...] += product

    @pl.when(step == pl.num_programs(0) - 1)
    def _():
        column_band = lax.broadcasted_iota(jnp.int32, (1, 4 * WIDTH), 1) % WIDTH // NOCC
        rows = jnp.zeros((NOCC, 4 * WIDTH), jnp.float32)
        for band in range(GROUP):
            rows = jnp.where(
                column_band == band, total[band * NOCC : (band + 1) * NOCC, :], rows
            )
        high = rows.astype(jnp.bfloat16)
        rest = rows - high.astype(jnp.float32)
        middle = rest.astype(jnp.bfloat16)
        low = (rest - middle.astype(jnp.float32)).astype(jnp.bfloat16)
        fold = fold_ref[...]
        parts = [
            jnp.dot(part, fold, preferred_element_type=jnp.float32)
            for part in (high, middle, low)
        ]
        out_ref[...] = (parts[0] + (parts[1] + parts[2])).T


def pair_terms(a, a_first, b, b_first, blocks, weights, fold):
    depth = a.shape[1]
    return pl.pallas_call(
        pair_kernel,
        grid=(blocks,),
        in_specs=[
            pl.BlockSpec((2, depth, WIDTH), lambda g: (0, 0, a_first + g)),
            pl.BlockSpec((2, depth, WIDTH), lambda g: (0, 0, b_first + g)),
            pl.BlockSpec((depth, 2), lambda g: (0, 0)),
            pl.BlockSpec((4 * WIDTH, 4 * NOCC), lambda g: (0, 0)),
        ],
        out_specs=pl.BlockSpec((4 * NOCC, NOCC), lambda g: (0, 0)),
        out_shape=jax.ShapeDtypeStruct((4 * NOCC, NOCC), jnp.float32),
        scratch_shapes=[
            pltpu.VMEM((2 * depth, 4 * WIDTH), jnp.bfloat16),
            pltpu.VMEM((WIDTH, 4 * WIDTH), jnp.float32),
        ],
        compiler_params=pltpu.CompilerParams(vmem_limit_bytes=32 * 2**20),
        cost_estimate=pl.CostEstimate(
            flops=2 * blocks * 2 * depth * 4 * WIDTH * WIDTH,
            bytes_accessed=blocks * 8 * depth * WIDTH,
            transcendentals=0,
        ),
        name="pair_terms",
    )(a, b, weights, fold)


def cut_kernel(at_ref, x_ref, out_ref):
    out_ref[...] = x_ref[...]


def cut(x, at):
    depth = x.shape[1]
    return pl.pallas_call(
        cut_kernel,
        grid_spec=pltpu.PrefetchScalarGridSpec(
            num_scalar_prefetch=1,
            grid=(2,),
            in_specs=[pl.BlockSpec((1, depth, WIDTH), lambda g, s: (g, 0, s[0]))],
            out_specs=pl.BlockSpec((1, depth, WIDTH), lambda g, s: (g, 0, 0)),
        ),
        out_shape=jax.ShapeDtypeStruct((2, depth, WIDTH), x.dtype),
        cost_estimate=pl.CostEstimate(
            flops=0, bytes_accessed=8 * depth * WIDTH, transcendentals=0
        ),
        name="cut",
    )(at.reshape(1), x)


def reduced(terms):
    owners, copies = lax.axis_size("band"), lax.axis_size("fit")
    rows = terms.shape[1]
    sent = jnp.broadcast_to(terms[:, None], (owners, copies, rows, NOCC))
    sent = sent.reshape(owners * copies, rows, NOCC)
    return lax.all_to_all(sent, ("band", "fit"), 0, 0, tiled=True).sum(0)


def by_owner(terms):
    owners = lax.axis_size("band")
    return terms.reshape(owners, 4 * NOCC // owners, NOCC)


def neighbours(distance, x, weights, fold):
    half = x.shape[2] // WIDTH // 2
    pieces = 2
    size = half // pieces
    foreign, own = 0, 0
    for piece in range(pieces):
        up_at, down_at = piece * size, half + piece * size
        below = shifted(x[:, :, up_at * WIDTH : (up_at + size) * WIDTH], "ka", 1)
        above = shifted(x[:, :, down_at * WIDTH : (down_at + size) * WIDTH], "ka", -1)
        if distance == 1:
            foreign += pair_terms(below, 0, x, up_at, size, weights, fold)
            own += pair_terms(x, down_at, above, 0, size, weights, fold)
        else:
            own += pair_terms(x, up_at, below, 0, size, weights, fold)
            foreign += pair_terms(above, 0, x, down_at, size, weights, fold)
    total = own + shifted(foreign, "ka", -1 if distance == 1 else 1)
    return reduced(by_owner(total))


def spread(distance, x, weights, fold):
    cycle = lax.axis_size("ka")
    far = cycle // 2
    me = lax.axis_index("ka")
    blocks = {0: cut(x, me)}
    order = [d for step in range(1, far) for d in (step, cycle - step)] + [far]
    for d in order:
        blocks[d] = shifted(cut(x, (me + cycle - d) % cycle), "ka", -d)
    late = [far, (far - distance) % cycle]
    early = [d for d in range(cycle) if d not in late]

    def terms(d):
        return by_owner(
            pair_terms(blocks[d], 0, blocks[(d + distance) % cycle], 0, 1, weights, fold)
        )

    def owned(pairs):
        parts = [terms(d) for d in pairs]
        rows = parts[0].shape[1]
        summed = reduced(jnp.concatenate(parts, axis=1))
        result = 0
        for at, d in enumerate(pairs):
            mine = summed[at * rows : (at + 1) * rows]
            result += shifted(mine, "ka", d) if d else mine
        return result

    first = owned(early)
    blocks[far], first = lax.optimization_barrier((blocks[far], first))
    return first + owned(late)


def shards(fitted, omega, coefficients, partner):
    cycle = lax.axis_size("ka")
    kernel = jnp.dot(
        coefficients, omega, precision=lax.Precision.HIGHEST, preferred_element_type=jnp.float32
    ) / math.sqrt(NAUX * NCABS)
    weights = kernel.T
    owners = lax.axis_size("band")
    fold = fold_matrix(owners)
    x = fitted[0]
    branches = [
        functools.partial(neighbours if distance in (1, cycle - 1) else spread, distance)
        for distance in range(1, cycle)
    ]
    total = lax.switch(partner[0] - 1, branches, x, weights, fold)
    total = total.reshape(2, 2, 1, NOCC // owners, NOCC)
    return (total[0], total[1])


def solution(mesh):
    placed = (P("ka", None, "fit", "band"), P(None, "fit"), P(), P())
    return jax.shard_map(
        shards,
        mesh=mesh,
        in_specs=placed,
        out_specs=(P(None, "ka", "band", None), P(None, "ka", "band", None)),
        check_vma=False,
    )
```

```python
import functools
import math

import jax
import jax.numpy as jnp
import numpy as np
from jax import lax
from jax.experimental import pallas as pl
from jax.experimental.pallas import tpu as pltpu
from jax.sharding import PartitionSpec as P

NOCC = 48
NCABS = 512
NAUX = 2048
GROUP = 8
WIDTH = GROUP * NOCC


def shifted(value, axis, by):
    devices = lax.axis_size(axis)
    return lax.ppermute(value, axis, [(i, (i + by) % devices) for i in range(devices)])


def fold_matrix(owners):
    rows = NOCC // owners
    column, row = np.arange(4 * WIDTH), np.arange(4 * NOCC)
    term, within = row % (4 * rows) // rows, row // (4 * rows) * rows + row % rows
    column_key = jnp.asarray(column // WIDTH * NOCC + column % NOCC, jnp.int32)
    row_key = jnp.asarray(term * NOCC + within, jnp.int32)
    return (column_key[:, None] == row_key[None, :]).astype(jnp.bfloat16)


def add_product(a_ref, b_ref, w_ref, scaled, total, begins):
    depth = w_ref.shape[0]
    rows = scaled.shape[0] // 2

    @pl.loop(0, depth // rows)
    def _(at):
        upper = pl.ds(pl.multiple_of(at * rows, rows), rows)
        lower = pl.ds(pl.multiple_of(depth + at * rows, rows), rows)
        real = a_ref[upper].astype(jnp.float32)
        imag = a_ref[lower].astype(jnp.float32)
        for operator in range(2):
            w = w_ref[upper, operator : operator + 1]
            a0 = (real * w).astype(jnp.bfloat16)
            a1 = (imag * w).astype(jnp.bfloat16)
            left = slice(2 * operator * WIDTH, (2 * operator + 1) * WIDTH)
            right = slice((2 * operator + 1) * WIDTH, (2 * operator + 2) * WIDTH)
            scaled[:rows, left] = a0
            scaled[rows:, left] = a1
            scaled[:rows, right] = a1
            scaled[rows:, right] = -a0
        before = jnp.where(begins & (at == 0), 0.0, total[...])
        total[...] = before + lax.dot_general(
            jnp.concatenate([b_ref[upper], b_ref[lower]]),
            scaled[...],
            (((0,), (0,)), ((), ())),
            preferred_element_type=jnp.float32,
        )


def folded_total(total, fold_ref):
    column_band = lax.broadcasted_iota(jnp.int32, (1, WIDTH), 1) // NOCC

    def add_term(term, result):
        columns = pl.ds(pl.multiple_of(term * WIDTH, WIDTH), WIDTH)
        diagonal = jnp.zeros((NOCC, WIDTH), jnp.float32)
        for band in range(GROUP):
            block = total[band * NOCC : (band + 1) * NOCC, columns]
            diagonal = jnp.where(column_band == band, block, diagonal)
        high = diagonal.astype(jnp.bfloat16)
        rest = diagonal - high.astype(jnp.float32)
        middle = rest.astype(jnp.bfloat16)
        low = (rest - middle.astype(jnp.float32)).astype(jnp.bfloat16)
        folded = jnp.dot(
            jnp.concatenate([high, middle, low]),
            fold_ref[columns, :],
            preferred_element_type=jnp.float32,
        )
        high, middle, low = (folded[n * NOCC : (n + 1) * NOCC] for n in range(3))
        return result + (high + (middle + low))

    zero = jnp.zeros((NOCC, 4 * NOCC), jnp.float32)
    return lax.fori_loop(0, 4, add_term, zero, unroll=True).T


A, B, SLOT, BEGINS, ENDS, A_COLUMN, B_COLUMN = range(7)


def list_kernel(places, pairs, *refs):
    arrays = len(refs) - 8
    w_ref, fold_ref, so_far_ref, out_ref, buffer, scaled, total, sems = refs[arrays:]
    step = pl.program_id(0)

    begin = jnp.where(step == 0, 0, 2 * step + 2)
    end = 2 * jnp.minimum(step + 2, pl.num_programs(0))

    @pl.loop(begin, end)
    def _(at):
        which, operand = at // 2, at % 2
        wanted = pairs[A + operand, which]
        column = pl.multiple_of(pairs[A_COLUMN + operand, which] * WIDTH, WIDTH)
        for place, (array, row) in enumerate(places):

            @pl.when(wanted == place)
            def _():
                pltpu.make_async_copy(
                    refs[array].at[pl.ds(row, buffer.shape[2]), pl.ds(column, WIDTH)],
                    buffer.at[which % 2, operand],
                    sems.at[which % 2, operand],
                ).start()

    slot = step % 2
    for operand in range(2):
        here = buffer.at[slot, operand]
        pltpu.make_async_copy(here, here, sems.at[slot, operand]).wait()
    begins = pairs[BEGINS, step] != 0
    add_product(buffer.at[slot, 0], buffer.at[slot, 1], w_ref, scaled, total, begins)

    @pl.when(pairs[ENDS, step] != 0)
    def _():
        terms = folded_total(total, fold_ref).reshape(out_ref.shape)
        out_ref[...] = so_far_ref[...] + terms


def list_terms(pairs, views, weights, fold, so_far):
    arrays = []
    places = []
    for array, row in views:
        known = [at for at, other in enumerate(arrays) if other is array]
        places.append((known[0] if known else len(arrays), row))
        if not known:
            arrays.append(array)
    owners, _, rows, _ = so_far.shape
    depth = weights.shape[0]
    block = pl.BlockSpec((owners, 1, rows, NOCC), lambda g, s: (0, s[SLOT, g], 0, 0))
    return pl.pallas_call(
        functools.partial(list_kernel, places),
        grid_spec=pltpu.PrefetchScalarGridSpec(
            num_scalar_prefetch=1,
            grid=(pairs.shape[1],),
            in_specs=[pl.BlockSpec(memory_space=pl.ANY)] * len(arrays)
            + [
                pl.BlockSpec((depth, 2), lambda g, s: (0, 0)),
                pl.BlockSpec((4 * WIDTH, 4 * NOCC), lambda g, s: (0, 0)),
                block,
            ],
            out_specs=block,
            scratch_shapes=[
                pltpu.VMEM((2, 2, 2 * depth, WIDTH), jnp.bfloat16),
                pltpu.VMEM((depth, 4 * WIDTH), jnp.bfloat16),
                pltpu.VMEM((WIDTH, 4 * WIDTH), jnp.float32),
                pltpu.SemaphoreType.DMA((2, 2)),
            ],
        ),
        out_shape=jax.ShapeDtypeStruct(so_far.shape, jnp.float32),
        input_output_aliases={len(arrays) + 3: 0},
        compiler_params=pltpu.CompilerParams(vmem_limit_bytes=32 * 2**20),
        cost_estimate=pl.CostEstimate(flops=0, bytes_accessed=0, transcendentals=0),
        name="list_terms",
    )(pairs, *arrays, weights, fold, so_far)


def cut_kernel(shifts, me_ref, x_ref, out_ref, sems):
    rows, columns = x_ref.shape
    copies = []
    for at, shift in enumerate(shifts):
        column = pl.multiple_of(lax.rem(me_ref[0] + shift, columns // WIDTH) * WIDTH, WIDTH)
        source = x_ref.at[:, pl.ds(column, WIDTH)]
        target = out_ref.at[pl.ds(at * rows, rows)]
        copies.append(pltpu.make_async_copy(source, target, sems.at[at]))
    for copy in copies:
        copy.start()
    for copy in copies:
        copy.wait()


def cut(x, me, shifts):
    rows = x.shape[0]
    return pl.pallas_call(
        functools.partial(cut_kernel, shifts),
        grid_spec=pltpu.PrefetchScalarGridSpec(
            num_scalar_prefetch=1,
            grid=(1,),
            in_specs=[pl.BlockSpec(memory_space=pl.ANY)],
            out_specs=pl.BlockSpec((rows * len(shifts), WIDTH), lambda g, me: (0, 0)),
            scratch_shapes=[pltpu.SemaphoreType.DMA((len(shifts),))],
        ),
        out_shape=jax.ShapeDtypeStruct((rows * len(shifts), WIDTH), x.dtype),
        compiler_params=pltpu.CompilerParams(vmem_limit_bytes=16 * 2**20),
        cost_estimate=pl.CostEstimate(flops=0, bytes_accessed=0, transcendentals=0),
        name="cut",
    )(me.reshape(1), x)


def reduced(terms):
    owners, copies = lax.axis_size("band"), lax.axis_size("fit")
    rows = terms.shape[1]
    sent = jnp.broadcast_to(terms[:, None], (owners, copies, rows, NOCC))
    sent = sent.reshape(owners * copies, rows, NOCC)
    return lax.all_to_all(sent, ("band", "fit"), 0, 0, tiled=True).sum(0)


def neighbours(distance, x, weights):
    owners = lax.axis_size("band")
    rows = 4 * NOCC // owners
    fold = fold_matrix(owners)
    half = x.shape[1] // WIDTH // 2
    sizes = [half - half // 4, half // 4]
    upward = distance == 1
    below, above = range(2)
    pieces = []
    at = 0
    for size in sizes:
        up = shifted(x[:, at * WIDTH : (at + size) * WIDTH], "ka", 1)
        down = shifted(x[:, (half + at) * WIDTH : (half + at + size) * WIDTH], "ka", -1)
        pieces.append((at, size, [(up, 0), (down, 0), (x, 0)]))
        at += size

    def table(at, size, foreign, slot):
        def columns(came, first):
            result = np.zeros((7, size), np.int32)
            place, column = (A, A_COLUMN) if foreign else (B, B_COLUMN)
            result[place], result[column] = came, np.arange(size)
            place, column = (B, B_COLUMN) if foreign else (A, A_COLUMN)
            result[place], result[column] = 2, first + np.arange(size)
            result[SLOT], result[BEGINS, 0], result[ENDS, -1] = slot, 1, 1
            return result

        upper, lower = columns(below, at), columns(above, half + at)
        return jnp.where(upward, *((upper, lower) if foreign else (lower, upper)))

    terms = jnp.zeros((owners, 2, rows, NOCC), jnp.float32)
    for at, size, views in pieces[:-1]:
        both = [table(at, size, True, 0), table(at, size, False, 1)]
        terms = list_terms(jnp.concatenate(both, axis=1), views, weights, fold, terms)
    foreign, own = terms[:, 0:1], terms[:, 1:2]
    at, size, views = pieces[-1]
    foreign = list_terms(table(at, size, True, 0), views, weights, fold, foreign)
    foreign, own = lax.optimization_barrier((foreign, own))
    own = list_terms(table(at, size, False, 0), views, weights, fold, own)
    own += shifted(jnp.where(upward, foreign, 0.0), "ka", -1)
    own += shifted(jnp.where(upward, 0.0, foreign), "ka", 1)
    return reduced(own[:, 0])


def listed_pairs(cycle, distance):
    far = cycle // 2

    def waits(d):
        blocks = (d, (d + distance) % cycle)
        return 2 if far - 1 in blocks or far + 1 in blocks else int(far in blocks)

    return sorted(range(cycle), key=lambda d: (waits(d), d))


def spread(distance, x, weights):
    owners = lax.axis_size("band")
    rows = 4 * NOCC // owners
    fold = fold_matrix(owners)
    cycle = lax.axis_size("ka")
    me = lax.axis_index("ka")
    size = x.shape[0]
    up_long, down_long = cut(x, me, [3]), cut(x, me, [cycle - 3])
    far = cut(x, me, [4])
    up_short, down_short = cut(x, me, [2, 1]), cut(x, me, [cycle - 2, cycle - 1])
    own = cut(x, me, [0])

    def ring(long, short, step):
        first = shifted(long, "ka", step)
        first, _, _ = lax.optimization_barrier((first, short, far))
        short = shifted(short, "ka", step)
        second = shifted(first, "ka", step)
        two = short[0:size]
        second, _ = lax.optimization_barrier((second, two))
        two = shifted(two, "ka", step)
        return short, two, shifted(second, "ka", step)

    up_short, up_two, up_long = ring(up_long, up_short, 1)
    down_short, down_two, down_long = ring(down_long, down_short, -1)
    far = shifted(far, "ka", 4)

    firsts = np.array([listed_pairs(cycle, max(t, 1)) for t in range(cycle)], np.int32)
    firsts = jnp.asarray(firsts)[distance]

    def table(first):
        one, none = jnp.ones_like(first), jnp.zeros_like(first)
        second, owner = (first + distance) % cycle, (first + me) % cycle
        return jnp.stack([first, second, owner, one, one, none, none])

    views = [
        (own, 0),
        (down_short, size),
        (down_two, 0),
        None,
        None,
        None,
        (up_two, 0),
        (up_short, size),
    ]
    soon = [(own, 0) if d in (3, 4, 5) else view for d, view in enumerate(views)]
    terms = jnp.zeros((owners, cycle, rows, NOCC), jnp.float32)
    terms = list_terms(table(firsts[:2]), soon, weights, fold, terms)
    far, terms = lax.optimization_barrier((far, terms))
    soon[4] = (far, 0)
    terms = list_terms(table(firsts[2:4]), soon, weights, fold, terms)
    up_long, down_long, terms = lax.optimization_barrier((up_long, down_long, terms))
    soon[3], soon[5] = (down_long, 0), (up_long, 0)
    terms = list_terms(table(firsts[4:]), soon, weights, fold, terms)
    mine = lax.all_to_all(terms, "band", 0, 0, tiled=True).sum(0)
    copies = lax.axis_size("fit")
    sent = jnp.broadcast_to(mine[:, None], (cycle, copies, rows, NOCC))
    sent = sent.reshape(cycle * copies, rows, NOCC)
    return lax.all_to_all(sent, ("ka", "fit"), 0, 0, tiled=True).sum(0)


def shards(fitted, omega, coefficients, partner):
    cycle = lax.axis_size("ka")
    kernel = jnp.dot(
        coefficients, omega, precision=lax.Precision.HIGHEST, preferred_element_type=jnp.float32
    ) / math.sqrt(NAUX * NCABS)
    weights = kernel.T
    owners = lax.axis_size("band")
    distance = partner[0]
    near = (distance == 1) | (distance == cycle - 1)
    x = fitted.reshape(2 * fitted.shape[2], fitted.shape[3])
    total = lax.cond(near, neighbours, spread, distance, x, weights)
    total = total.reshape(2, 2, 1, NOCC // owners, NOCC)
    return (total[0], total[1])


def solution(mesh):
    placed = (P("ka", None, "fit", "band"), P(None, "fit"), P(), P())
    return jax.shard_map(
        shards,
        mesh=mesh,
        in_specs=placed,
        out_specs=(P(None, "ka", "band", None), P(None, "ka", "band", None)),
        check_vma=False,
    )
```

```python
import functools
import math

import jax
import jax.numpy as jnp
import numpy as np
from jax import lax
from jax.experimental import pallas as pl
from jax.experimental.pallas import tpu as pltpu
from jax.sharding import PartitionSpec as P

NOCC = 48
NCABS = 512
NAUX = 2048
GROUP = 8
WIDTH = GROUP * NOCC


def shifted(value, axis, by):
    devices = lax.axis_size(axis)
    return lax.ppermute(value, axis, [(i, (i + by) % devices) for i in range(devices)])


def fold_matrix(owners):
    rows = NOCC // owners
    column, row = np.arange(4 * WIDTH), np.arange(4 * NOCC)
    term, within = row % (4 * rows) // rows, row // (4 * rows) * rows + row % rows
    column_key = jnp.asarray(column // WIDTH * NOCC + column % NOCC, jnp.int32)
    row_key = jnp.asarray(term * NOCC + within, jnp.int32)
    return (column_key[:, None] == row_key[None, :]).astype(jnp.bfloat16)


def add_product(a_ref, b_ref, w_ref, scaled, total, begins):
    depth = w_ref.shape[0]
    rows = scaled.shape[0] // 2

    @pl.loop(0, depth // rows)
    def _(at):
        upper = pl.ds(pl.multiple_of(at * rows, rows), rows)
        lower = pl.ds(pl.multiple_of(depth + at * rows, rows), rows)
        real = a_ref[upper].astype(jnp.float32)
        imag = a_ref[lower].astype(jnp.float32)
        for operator in range(2):
            w = w_ref[upper, operator : operator + 1]
            a0 = (real * w).astype(jnp.bfloat16)
            a1 = (imag * w).astype(jnp.bfloat16)
            left = slice(2 * operator * WIDTH, (2 * operator + 1) * WIDTH)
            right = slice((2 * operator + 1) * WIDTH, (2 * operator + 2) * WIDTH)
            scaled[:rows, left] = a0
            scaled[rows:, left] = a1
            scaled[:rows, right] = a1
            scaled[rows:, right] = -a0
        before = jnp.where(begins & (at == 0), 0.0, total[...])
        total[...] = before + lax.dot_general(
            jnp.concatenate([b_ref[upper], b_ref[lower]]),
            scaled[...],
            (((0,), (0,)), ((), ())),
            preferred_element_type=jnp.float32,
        )


def folded_total(total, fold_ref):
    column_band = lax.broadcasted_iota(jnp.int32, (1, WIDTH), 1) // NOCC

    def add_term(term, result):
        columns = pl.ds(pl.multiple_of(term * WIDTH, WIDTH), WIDTH)
        diagonal = jnp.zeros((NOCC, WIDTH), jnp.float32)
        for band in range(GROUP):
            block = total[band * NOCC : (band + 1) * NOCC, columns]
            diagonal = jnp.where(column_band == band, block, diagonal)
        high = diagonal.astype(jnp.bfloat16)
        rest = diagonal - high.astype(jnp.float32)
        middle = rest.astype(jnp.bfloat16)
        low = (rest - middle.astype(jnp.float32)).astype(jnp.bfloat16)
        folded = jnp.dot(
            jnp.concatenate([high, middle, low]),
            fold_ref[columns, :],
            preferred_element_type=jnp.float32,
        )
        high, middle, low = (folded[n * NOCC : (n + 1) * NOCC] for n in range(3))
        return result + (high + (middle + low))

    zero = jnp.zeros((NOCC, 4 * NOCC), jnp.float32)
    return lax.fori_loop(0, 4, add_term, zero, unroll=True).T


A, B, SLOT, BEGINS, ENDS, A_COLUMN, B_COLUMN = range(7)


def list_kernel(places, pairs, *refs):
    arrays = len(refs) - 8
    w_ref, fold_ref, so_far_ref, out_ref, buffer, scaled, total, sems = refs[arrays:]
    step = pl.program_id(0)

    begin = jnp.where(step == 0, 0, 2 * step + 2)
    end = 2 * jnp.minimum(step + 2, pl.num_programs(0))

    @pl.loop(begin, end)
    def _(at):
        which, operand = at // 2, at % 2
        wanted = pairs[A + operand, which]
        column = pl.multiple_of(pairs[A_COLUMN + operand, which] * WIDTH, WIDTH)
        for place, parts in enumerate(places):

            @pl.when(wanted == place)
            def _():
                rows = buffer.shape[2] // len(parts)
                for at, (array, row) in enumerate(parts):
                    pltpu.make_async_copy(
                        refs[array].at[pl.ds(row, rows), pl.ds(column, WIDTH)],
                        buffer.at[which % 2, operand, pl.ds(at * rows, rows)],
                        sems.at[which % 2, operand],
                    ).start()

    slot = step % 2
    for operand in range(2):
        here = buffer.at[slot, operand]
        pltpu.make_async_copy(here, here, sems.at[slot, operand]).wait()
    begins = pairs[BEGINS, step] != 0
    add_product(buffer.at[slot, 0], buffer.at[slot, 1], w_ref, scaled, total, begins)

    @pl.when(pairs[ENDS, step] != 0)
    def _():
        terms = folded_total(total, fold_ref).reshape(out_ref.shape)
        out_ref[...] = so_far_ref[...] + terms


def list_terms(pairs, views, weights, fold, so_far):
    arrays = []
    places = []
    for parts in views:
        place = []
        for array, row in parts:
            known = [at for at, other in enumerate(arrays) if other is array]
            place.append((known[0] if known else len(arrays), row))
            if not known:
                arrays.append(array)
        places.append(place)
    _, owners, rows, _ = so_far.shape
    depth = weights.shape[0]
    block = pl.BlockSpec((1, owners, rows, NOCC), lambda g, s: (s[SLOT, g], 0, 0, 0))
    return pl.pallas_call(
        functools.partial(list_kernel, places),
        grid_spec=pltpu.PrefetchScalarGridSpec(
            num_scalar_prefetch=1,
            grid=(pairs.shape[1],),
            in_specs=[pl.BlockSpec(memory_space=pl.ANY)] * len(arrays)
            + [
                pl.BlockSpec((depth, 2), lambda g, s: (0, 0)),
                pl.BlockSpec((4 * WIDTH, 4 * NOCC), lambda g, s: (0, 0)),
                block,
            ],
            out_specs=block,
            scratch_shapes=[
                pltpu.VMEM((2, 2, 2 * depth, WIDTH), jnp.bfloat16),
                pltpu.VMEM((depth, 4 * WIDTH), jnp.bfloat16),
                pltpu.VMEM((WIDTH, 4 * WIDTH), jnp.float32),
                pltpu.SemaphoreType.DMA((2, 2)),
            ],
        ),
        out_shape=jax.ShapeDtypeStruct(so_far.shape, jnp.float32),
        input_output_aliases={len(arrays) + 3: 0},
        compiler_params=pltpu.CompilerParams(vmem_limit_bytes=32 * 2**20),
        cost_estimate=pl.CostEstimate(flops=0, bytes_accessed=0, transcendentals=0),
        name="list_terms",
    )(pairs, *arrays, weights, fold, so_far)


def cut_kernel(groups, me_ref, x_ref, *refs):
    *out_refs, sems = refs
    columns = x_ref.shape[1] // WIDTH
    copies = []
    for pieces, out_ref in zip(groups, out_refs):
        row = 0
        for shift, begin, rows in pieces:
            column = pl.multiple_of(lax.rem(me_ref[0] + shift, columns) * WIDTH, WIDTH)
            source = x_ref.at[pl.ds(begin, rows), pl.ds(column, out_ref.shape[1])]
            target = out_ref.at[pl.ds(row, rows)]
            copies.append(pltpu.make_async_copy(source, target, sems.at[len(copies)]))
            row += rows
    for copy in copies:
        copy.start()
    for copy in copies:
        copy.wait()


def cut(x, me, *groups, blocks=1):
    shapes = [(sum(rows for _, _, rows in pieces), blocks * WIDTH) for pieces in groups]
    count = sum(len(pieces) for pieces in groups)
    return pl.pallas_call(
        functools.partial(cut_kernel, groups),
        grid_spec=pltpu.PrefetchScalarGridSpec(
            num_scalar_prefetch=1,
            grid=(1,),
            in_specs=[pl.BlockSpec(memory_space=pl.ANY)],
            out_specs=[pl.BlockSpec(shape, lambda g, me: (0, 0)) for shape in shapes],
            scratch_shapes=[pltpu.SemaphoreType.DMA((count,))],
        ),
        out_shape=[jax.ShapeDtypeStruct(shape, x.dtype) for shape in shapes],
        compiler_params=pltpu.CompilerParams(vmem_limit_bytes=32 * 2**20),
        cost_estimate=pl.CostEstimate(flops=0, bytes_accessed=0, transcendentals=0),
        name="cut",
    )(me.reshape(1), x)


def weights_of(coefficients, omega):
    kernel = jnp.dot(
        coefficients, omega, precision=lax.Precision.HIGHEST, preferred_element_type=jnp.float32
    ) / math.sqrt(NAUX * NCABS)
    return kernel.T


def reduced(terms):
    owners, copies = lax.axis_size("band"), lax.axis_size("fit")
    rows = terms.shape[1]
    sent = jnp.broadcast_to(terms[:, None], (owners, copies, rows, NOCC))
    sent = sent.reshape(owners * copies, rows, NOCC)
    return lax.all_to_all(sent, ("band", "fit"), 0, 0, tiled=True).sum(0)


def neighbours(distance, x, coefficients, omega):
    owners = lax.axis_size("band")
    rows = 4 * NOCC // owners
    fold = fold_matrix(owners)
    weights = weights_of(coefficients, omega)
    height = x.shape[0]
    half = x.shape[1] // WIDTH // 2
    upward = distance == 1
    start = jnp.zeros((), jnp.int32)
    pieces = []
    at = 0
    for size in (half - half // 4, half // 4):
        low, high = [(at, 0, height)], [(half + at, 0, height)]
        up, down = cut(x, start, low, high, blocks=size)
        views = [[(shifted(up, "ka", 1), 0)], [(shifted(down, "ka", -1), 0)], [(x, 0)]]
        pieces.append((at, size, views))
        at += size

    def table(at, size, foreign):
        def columns(came, first):
            result = np.zeros((7, size), np.int32)
            place, column = (A, A_COLUMN) if foreign else (B, B_COLUMN)
            result[place], result[column] = came, np.arange(size)
            place, column = (B, B_COLUMN) if foreign else (A, A_COLUMN)
            result[place], result[column] = 2, first + np.arange(size)
            result[SLOT], result[BEGINS, 0], result[ENDS, -1] = int(foreign), 1, 1
            return result

        up, down = columns(0, at), columns(1, half + at)
        return jnp.where(upward, *((up, down) if foreign else (down, up)))

    terms = jnp.zeros((2, owners, rows, NOCC), jnp.float32)
    for at, size, views in pieces:
        pairs = jnp.concatenate([table(at, size, True), table(at, size, False)], axis=1)
        terms = list_terms(pairs, views, weights, fold, terms)
    own, foreign = terms[0], terms[1]
    own += shifted(jnp.where(upward, foreign, 0.0), "ka", -1)
    own += shifted(jnp.where(upward, 0.0, foreign), "ka", 1)
    return reduced(own)


def listed_pairs(cycle, distance):
    far = cycle // 2

    def waits(d):
        blocks = (d, (d + distance) % cycle)
        return 2 if far in blocks else int(2 in blocks or cycle - 2 in blocks)

    return sorted(range(cycle), key=lambda d: (waits(d), d))


def spread(distance, x, coefficients, omega):
    owners = lax.axis_size("band")
    rows = 4 * NOCC // owners
    fold = fold_matrix(owners)
    weights = weights_of(coefficients, omega)
    cycle = lax.axis_size("ka")
    me = lax.axis_index("ka")
    size = x.shape[0]
    part = size // 2

    def whole(d):
        return (d % cycle, 0, size)

    up_long, down_long = cut(
        x, me, [whole(3), (4, 0, part)], [whole(-3), (4, part, part)]
    )
    up_short, down_short = cut(x, me, [whole(2), whole(1)], [whole(-2), whole(-1)])
    own = cut(x, me, [whole(0)])[0]

    def ring(long, short, step):
        first = shifted(long, "ka", step)
        first, _ = lax.optimization_barrier((first, short))
        short = shifted(short, "ka", step)
        second = shifted(first, "ka", step)
        third = shifted(second, "ka", step)
        return short, shifted(short[:size], "ka", step), third, shifted(third[size:], "ka", step)

    up_short, up_two, up_long, up_far = ring(up_long, up_short, 1)
    down_short, down_two, down_long, down_far = ring(down_long, down_short, -1)

    firsts = np.array([listed_pairs(cycle, max(t, 1)) for t in range(cycle)], np.int32)
    firsts = jnp.asarray(firsts)[distance]

    def table(first):
        one, none = jnp.ones_like(first), jnp.zeros_like(first)
        second, owner = (first + distance) % cycle, (first + me) % cycle
        return jnp.stack([first, second, owner, one, one, none, none])

    views = [[(own, 0)]] * cycle
    views[1], views[7] = [(down_short, size)], [(up_short, size)]
    views[3], views[5] = [(down_long, 0)], [(up_long, 0)]
    terms = jnp.zeros((cycle, owners, rows, NOCC), jnp.float32)
    terms = list_terms(table(firsts[:2]), views, weights, fold, terms)
    up_two, down_two, terms = lax.optimization_barrier((up_two, down_two, terms))
    views[2], views[6] = [(down_two, 0)], [(up_two, 0)]
    terms = list_terms(table(firsts[2:6]), views, weights, fold, terms)
    up_far, down_far, terms = lax.optimization_barrier((up_far, down_far, terms))
    views[4] = [(up_far, 0), (down_far, 0)]
    terms = list_terms(table(firsts[6:]), views, weights, fold, terms)
    sent = terms.reshape(cycle * owners, rows, NOCC)
    mine = lax.all_to_all(sent, ("ka", "band"), 0, 0, tiled=True).sum(0)
    return lax.all_gather(mine, "fit").sum(0)


def shards(fitted, omega, coefficients, partner):
    cycle = lax.axis_size("ka")
    distance = partner[0]
    away = (distance != 1) & (distance != cycle - 1)
    x = fitted.reshape(2 * fitted.shape[2], fitted.shape[3])
    total = lax.cond(away, spread, neighbours, distance, x, coefficients, omega)
    total = total.reshape(2, 2, 1, -1, NOCC)
    return (total[0], total[1])


def solution(mesh):
    placed = (P("ka", None, "fit", "band"), P(None, "fit"), P(), P())
    return jax.shard_map(
        shards,
        mesh=mesh,
        in_specs=placed,
        out_specs=(P(None, "ka", "band", None), P(None, "ka", "band", None)),
        check_vma=False,
    )
```

```python
import functools
import math

import jax
import jax.numpy as jnp
import numpy as np
from jax import lax
from jax.experimental import pallas as pl
from jax.experimental.pallas import tpu as pltpu
from jax.sharding import PartitionSpec as P

NOCC = 48
NCABS = 512
NAUX = 2048
GROUP = 8
WIDTH = GROUP * NOCC


def shifted(value, axis, by):
    devices = lax.axis_size(axis)
    return lax.ppermute(value, axis, [(i, (i + by) % devices) for i in range(devices)])


def fold_matrix(owners):
    rows = NOCC // owners
    column, row = np.arange(4 * WIDTH), np.arange(4 * NOCC)
    term, within = row % (4 * rows) // rows, row // (4 * rows) * rows + row % rows
    column_key = jnp.asarray(column // WIDTH * NOCC + column % NOCC, jnp.int32)
    row_key = jnp.asarray(term * NOCC + within, jnp.int32)
    return (column_key[:, None] == row_key[None, :]).astype(jnp.bfloat16)


def add_product(a_ref, b_ref, w_ref, scaled, total, begins):
    depth = w_ref.shape[0]
    rows = scaled.shape[0] // 2

    @pl.loop(0, depth // rows)
    def _(at):
        upper = pl.ds(pl.multiple_of(at * rows, rows), rows)
        lower = pl.ds(pl.multiple_of(depth + at * rows, rows), rows)
        real = a_ref[upper].astype(jnp.float32)
        imag = a_ref[lower].astype(jnp.float32)
        for operator in range(2):
            w = w_ref[upper, operator : operator + 1]
            a0 = (real * w).astype(jnp.bfloat16)
            a1 = (imag * w).astype(jnp.bfloat16)
            left = slice(2 * operator * WIDTH, (2 * operator + 1) * WIDTH)
            right = slice((2 * operator + 1) * WIDTH, (2 * operator + 2) * WIDTH)
            scaled[:rows, left] = a0
            scaled[rows:, left] = a1
            scaled[:rows, right] = a1
            scaled[rows:, right] = -a0
        before = jnp.where(begins & (at == 0), 0.0, total[...])
        total[...] = before + lax.dot_general(
            jnp.concatenate([b_ref[upper], b_ref[lower]]),
            scaled[...],
            (((0,), (0,)), ((), ())),
            preferred_element_type=jnp.float32,
        )


def folded_total(total, fold_ref):
    column_band = lax.broadcasted_iota(jnp.int32, (1, WIDTH), 1) // NOCC

    def add_term(term, result):
        columns = pl.ds(pl.multiple_of(term * WIDTH, WIDTH), WIDTH)
        diagonal = jnp.zeros((NOCC, WIDTH), jnp.float32)
        for band in range(GROUP):
            block = total[band * NOCC : (band + 1) * NOCC, columns]
            diagonal = jnp.where(column_band == band, block, diagonal)
        high = diagonal.astype(jnp.bfloat16)
        rest = diagonal - high.astype(jnp.float32)
        middle = rest.astype(jnp.bfloat16)
        low = (rest - middle.astype(jnp.float32)).astype(jnp.bfloat16)
        folded = jnp.dot(
            jnp.concatenate([high, middle, low]),
            fold_ref[columns, :],
            preferred_element_type=jnp.float32,
        )
        high, middle, low = (folded[n * NOCC : (n + 1) * NOCC] for n in range(3))
        return result + (high + (middle + low))

    zero = jnp.zeros((NOCC, 4 * NOCC), jnp.float32)
    return lax.fori_loop(0, 4, add_term, zero, unroll=True).T


A, B, SLOT, BEGINS, ENDS, A_COLUMN, B_COLUMN = range(7)


def list_kernel(places, pairs, *refs):
    arrays = len(refs) - 8
    w_ref, fold_ref, so_far_ref, out_ref, buffer, scaled, total, sems = refs[arrays:]
    step = pl.program_id(0)

    begin = jnp.where(step == 0, 0, 2 * step + 2)
    end = 2 * jnp.minimum(step + 2, pl.num_programs(0))

    @pl.loop(begin, end)
    def _(at):
        which, operand = at // 2, at % 2
        wanted = pairs[A + operand, which]
        column = pl.multiple_of(pairs[A_COLUMN + operand, which] * WIDTH, WIDTH)
        for place, parts in enumerate(places):

            @pl.when(wanted == place)
            def _():
                rows = buffer.shape[2] // len(parts)
                for at, (array, row) in enumerate(parts):
                    pltpu.make_async_copy(
                        refs[array].at[pl.ds(row, rows), pl.ds(column, WIDTH)],
                        buffer.at[which % 2, operand, pl.ds(at * rows, rows)],
                        sems.at[which % 2, operand],
                    ).start()

    @pl.when(pairs[A, step] >= 0)
    def _():
        slot = step % 2
        for operand in range(2):
            here = buffer.at[slot, operand]
            pltpu.make_async_copy(here, here, sems.at[slot, operand]).wait()
        begins = pairs[BEGINS, step] != 0
        add_product(buffer.at[slot, 0], buffer.at[slot, 1], w_ref, scaled, total, begins)

    @pl.when((pairs[A, step] >= 0) & (pairs[ENDS, step] != 0))
    def _():
        terms = folded_total(total, fold_ref).reshape(out_ref.shape)
        out_ref[...] = so_far_ref[...] + terms


def list_terms(pairs, views, weights, fold, so_far):
    arrays = []
    places = []
    for parts in views:
        place = []
        for array, row in parts:
            known = [at for at, other in enumerate(arrays) if other is array]
            place.append((known[0] if known else len(arrays), row))
            if not known:
                arrays.append(array)
        places.append(place)
    _, owners, rows, _ = so_far.shape
    depth = weights.shape[0]
    block = pl.BlockSpec((1, owners, rows, NOCC), lambda g, s: (s[SLOT, g], 0, 0, 0))
    return pl.pallas_call(
        functools.partial(list_kernel, places),
        grid_spec=pltpu.PrefetchScalarGridSpec(
            num_scalar_prefetch=1,
            grid=(pairs.shape[1],),
            in_specs=[pl.BlockSpec(memory_space=pl.ANY)] * len(arrays)
            + [
                pl.BlockSpec((depth, 2), lambda g, s: (0, 0)),
                pl.BlockSpec((4 * WIDTH, 4 * NOCC), lambda g, s: (0, 0)),
                block,
            ],
            out_specs=block,
            scratch_shapes=[
                pltpu.VMEM((2, 2, 2 * depth, WIDTH), jnp.bfloat16),
                pltpu.VMEM((depth, 4 * WIDTH), jnp.bfloat16),
                pltpu.VMEM((WIDTH, 4 * WIDTH), jnp.float32),
                pltpu.SemaphoreType.DMA((2, 2)),
            ],
        ),
        out_shape=jax.ShapeDtypeStruct(so_far.shape, jnp.float32),
        input_output_aliases={len(arrays) + 3: 0},
        compiler_params=pltpu.CompilerParams(vmem_limit_bytes=32 * 2**20),
        cost_estimate=pl.CostEstimate(flops=0, bytes_accessed=0, transcendentals=0),
        name="list_terms",
    )(pairs, *arrays, weights, fold, so_far)


def cut_kernel(groups, me_ref, x_ref, *refs):
    *out_refs, sems = refs
    columns = x_ref.shape[1] // WIDTH
    copies = []
    for pieces, out_ref in zip(groups, out_refs):
        row = 0
        for shift, begin, rows in pieces:
            column = pl.multiple_of(lax.rem(me_ref[0] + shift, columns) * WIDTH, WIDTH)
            source = x_ref.at[pl.ds(begin, rows), pl.ds(column, out_ref.shape[1])]
            target = out_ref.at[pl.ds(row, rows)]
            copies.append(pltpu.make_async_copy(source, target, sems.at[len(copies)]))
            row += rows
    for copy in copies:
        copy.start()
    for copy in copies:
        copy.wait()


def cut(x, me, *groups, blocks=1):
    shapes = [(sum(rows for _, _, rows in pieces), blocks * WIDTH) for pieces in groups]
    count = sum(len(pieces) for pieces in groups)
    return pl.pallas_call(
        functools.partial(cut_kernel, groups),
        grid_spec=pltpu.PrefetchScalarGridSpec(
            num_scalar_prefetch=1,
            grid=(1,),
            in_specs=[pl.BlockSpec(memory_space=pl.ANY)],
            out_specs=[pl.BlockSpec(shape, lambda g, me: (0, 0)) for shape in shapes],
            scratch_shapes=[pltpu.SemaphoreType.DMA((count,))],
        ),
        out_shape=[jax.ShapeDtypeStruct(shape, x.dtype) for shape in shapes],
        compiler_params=pltpu.CompilerParams(vmem_limit_bytes=32 * 2**20),
        cost_estimate=pl.CostEstimate(flops=0, bytes_accessed=0, transcendentals=0),
        name="cut",
    )(me.reshape(1), x)


def weights_of(coefficients, omega):
    kernel = jnp.dot(
        coefficients, omega, precision=lax.Precision.HIGHEST, preferred_element_type=jnp.float32
    ) / math.sqrt(NAUX * NCABS)
    return kernel.T


def reduced(terms):
    owners, copies = lax.axis_size("band"), lax.axis_size("fit")
    rows = terms.shape[1]
    sent = jnp.broadcast_to(terms[:, None], (owners, copies, rows, NOCC))
    sent = sent.reshape(owners * copies, rows, NOCC)
    return lax.all_to_all(sent, ("band", "fit"), 0, 0, tiled=True).sum(0)


def neighbours(distance, x, coefficients, omega):
    owners = lax.axis_size("band")
    rows = 4 * NOCC // owners
    fold = fold_matrix(owners)
    weights = weights_of(coefficients, omega)
    height = x.shape[0]
    half = x.shape[1] // WIDTH // 2
    upward = distance == 1
    start = jnp.zeros((), jnp.int32)
    pieces = []
    at = 0
    for size in (half - half // 4, half // 4):
        low, high = [(at, 0, height)], [(half + at, 0, height)]
        up, down = cut(x, start, low, high, blocks=size)
        views = [[(shifted(up, "ka", 1), 0)], [(shifted(down, "ka", -1), 0)], [(x, 0)]]
        pieces.append((at, size, views))
        at += size

    def table(at, size, foreign):
        def columns(came, first):
            result = np.zeros((7, size), np.int32)
            place, column = (A, A_COLUMN) if foreign else (B, B_COLUMN)
            result[place], result[column] = came, np.arange(size)
            place, column = (B, B_COLUMN) if foreign else (A, A_COLUMN)
            result[place], result[column] = 2, first + np.arange(size)
            result[SLOT], result[BEGINS, 0], result[ENDS, -1] = int(foreign), 1, 1
            return result

        up, down = columns(0, at), columns(1, half + at)
        return jnp.where(upward, *((up, down) if foreign else (down, up)))

    terms = jnp.zeros((2, owners, rows, NOCC), jnp.float32)
    for at, size, views in pieces:
        pairs = jnp.concatenate([table(at, size, True), table(at, size, False)], axis=1)
        terms = list_terms(pairs, views, weights, fold, terms)
    own, foreign = terms[0], terms[1]
    own += shifted(jnp.where(upward, foreign, 0.0), "ka", -1)
    own += shifted(jnp.where(upward, 0.0, foreign), "ka", 1)
    return reduced(own)


def listed_pairs(cycle, distance):
    far = cycle // 2
    groups = [[], [], []]
    for d in range(cycle):
        blocks = (d, (d + distance) % cycle)
        late = 2 if far in blocks else int(2 in blocks or cycle - 2 in blocks)
        groups[late].append((*blocks, d))
    steps = []
    for group, length in zip(groups, (4, 4, 2)):
        idle = (-1, -1, group[-1][2])
        steps += group + [idle] * (length - len(group))
    return np.array(steps, np.int32).T


def spread(distance, x, coefficients, omega):
    owners = lax.axis_size("band")
    rows = 4 * NOCC // owners
    fold = fold_matrix(owners)
    weights = weights_of(coefficients, omega)
    cycle = lax.axis_size("ka")
    me = lax.axis_index("ka")
    size = x.shape[0]
    part = size // 2

    def whole(d):
        return (d % cycle, 0, size)

    up_long, down_long = cut(
        x, me, [whole(3), (4, 0, part)], [whole(-3), (4, part, part)]
    )
    up_short, down_short = cut(x, me, [whole(2), whole(1)], [whole(-2), whole(-1)])
    own = cut(x, me, [whole(0)])[0]

    def ring(long, short, step):
        first = shifted(long, "ka", step)
        first, _ = lax.optimization_barrier((first, short))
        short = shifted(short, "ka", step)
        second = shifted(first, "ka", step)
        third = shifted(second, "ka", step)
        return short, shifted(short[:size], "ka", step), third, shifted(third[size:], "ka", step)

    up_short, up_two, up_long, up_far = ring(up_long, up_short, 1)
    down_short, down_two, down_long, down_far = ring(down_long, down_short, -1)

    listed = np.stack([listed_pairs(cycle, min(max(t, 2), cycle - 2)) for t in range(cycle)])
    listed = jnp.asarray(listed)[distance]

    def table(begin, end):
        first, second, place = listed[:, begin:end]
        one, none = jnp.ones_like(first), jnp.zeros_like(first)
        return jnp.stack([first, second, (place + me) % cycle, one, one, none, none])

    views = [[(own, 0)]] * cycle
    views[1], views[7] = [(down_short, size)], [(up_short, size)]
    views[3], views[5] = [(down_long, 0)], [(up_long, 0)]
    terms = jnp.zeros((cycle, owners, rows, NOCC), jnp.float32)
    terms = list_terms(table(0, 4), views, weights, fold, terms)
    up_two, down_two, terms = lax.optimization_barrier((up_two, down_two, terms))
    views[2], views[6] = [(down_two, 0)], [(up_two, 0)]
    terms = list_terms(table(4, 8), views, weights, fold, terms)
    up_far, down_far, terms = lax.optimization_barrier((up_far, down_far, terms))
    views[4] = [(up_far, 0), (down_far, 0)]
    terms = list_terms(table(8, 10), views, weights, fold, terms)
    sent = terms.reshape(cycle * owners, rows, NOCC)
    mine = lax.all_to_all(sent, ("ka", "band"), 0, 0, tiled=True).sum(0)
    return lax.all_gather(mine, "fit").sum(0)


def shards(fitted, omega, coefficients, partner):
    cycle = lax.axis_size("ka")
    distance = partner[0]
    away = (distance != 1) & (distance != cycle - 1)
    x = fitted.reshape(2 * fitted.shape[2], fitted.shape[3])
    total = lax.cond(away, spread, neighbours, distance, x, coefficients, omega)
    total = total.reshape(2, 2, 1, -1, NOCC)
    return (total[0], total[1])


def solution(mesh):
    placed = (P("ka", None, "fit", "band"), P(None, "fit"), P(), P())
    return jax.shard_map(
        shards,
        mesh=mesh,
        in_specs=placed,
        out_specs=(P(None, "ka", "band", None), P(None, "ka", "band", None)),
        check_vma=False,
    )
```

```python
import functools
import math

import jax
import jax.numpy as jnp
import numpy as np
from jax import lax
from jax.experimental import pallas as pl
from jax.experimental.pallas import tpu as pltpu
from jax.sharding import PartitionSpec as P

NOCC = 48
NCABS = 512
NAUX = 2048
GROUP = 8
WIDTH = GROUP * NOCC


def shifted(value, axis, by):
    devices = lax.axis_size(axis)
    return lax.ppermute(value, axis, [(i, (i + by) % devices) for i in range(devices)])


def fold_matrix(owners):
    rows = NOCC // owners
    column, row = np.arange(4 * WIDTH), np.arange(4 * NOCC)
    term, within = row % (4 * rows) // rows, row // (4 * rows) * rows + row % rows
    column_key = jnp.asarray(column // WIDTH * NOCC + column % NOCC, jnp.int32)
    row_key = jnp.asarray(term * NOCC + within, jnp.int32)
    return (column_key[:, None] == row_key[None, :]).astype(jnp.bfloat16)


def add_product(a_ref, b_ref, w_ref, scaled, total, begins):
    depth = w_ref.shape[0]
    rows = scaled.shape[0] // 2

    @pl.loop(0, depth // rows)
    def _(at):
        upper = pl.ds(pl.multiple_of(at * rows, rows), rows)
        lower = pl.ds(pl.multiple_of(depth + at * rows, rows), rows)
        real = a_ref[upper].astype(jnp.float32)
        imag = a_ref[lower].astype(jnp.float32)
        for operator in range(2):
            w = w_ref[upper, operator : operator + 1]
            a0 = (real * w).astype(jnp.bfloat16)
            a1 = (imag * w).astype(jnp.bfloat16)
            left = slice(2 * operator * WIDTH, (2 * operator + 1) * WIDTH)
            right = slice((2 * operator + 1) * WIDTH, (2 * operator + 2) * WIDTH)
            scaled[:rows, left] = a0
            scaled[rows:, left] = a1
            scaled[:rows, right] = a1
            scaled[rows:, right] = -a0
        before = jnp.where(begins & (at == 0), 0.0, total[...])
        total[...] = before + lax.dot_general(
            jnp.concatenate([b_ref[upper], b_ref[lower]]),
            scaled[...],
            (((0,), (0,)), ((), ())),
            preferred_element_type=jnp.float32,
        )


def folded_total(total, fold_ref):
    column_band = lax.broadcasted_iota(jnp.int32, (1, WIDTH), 1) // NOCC

    def add_term(term, result):
        columns = pl.ds(pl.multiple_of(term * WIDTH, WIDTH), WIDTH)
        diagonal = jnp.zeros((NOCC, WIDTH), jnp.float32)
        for band in range(GROUP):
            block = total[band * NOCC : (band + 1) * NOCC, columns]
            diagonal = jnp.where(column_band == band, block, diagonal)
        high = diagonal.astype(jnp.bfloat16)
        rest = diagonal - high.astype(jnp.float32)
        middle = rest.astype(jnp.bfloat16)
        low = (rest - middle.astype(jnp.float32)).astype(jnp.bfloat16)
        folded = jnp.dot(
            jnp.concatenate([high, middle, low]),
            fold_ref[columns, :],
            preferred_element_type=jnp.float32,
        )
        high, middle, low = (folded[n * NOCC : (n + 1) * NOCC] for n in range(3))
        return result + (high + (middle + low))

    zero = jnp.zeros((NOCC, 4 * NOCC), jnp.float32)
    return lax.fori_loop(0, 4, add_term, zero, unroll=True).T


A, B, SLOT, BEGINS, ENDS, A_COLUMN, B_COLUMN = range(7)


def list_kernel(places, pairs, *refs):
    arrays = len(refs) - 8
    w_ref, fold_ref, so_far_ref, out_ref, buffer, scaled, total, sems = refs[arrays:]
    step = pl.program_id(0)

    begin = jnp.where(step == 0, 0, 2 * step + 2)
    end = 2 * jnp.minimum(step + 2, pl.num_programs(0))

    @pl.loop(begin, end)
    def _(at):
        which, operand = at // 2, at % 2
        wanted = pairs[A + operand, which]
        column = pl.multiple_of(pairs[A_COLUMN + operand, which] * WIDTH, WIDTH)
        for place, parts in enumerate(places):

            @pl.when(wanted == place)
            def _():
                rows = buffer.shape[2] // len(parts)
                for at, (array, row) in enumerate(parts):
                    pltpu.make_async_copy(
                        refs[array].at[pl.ds(row, rows), pl.ds(column, WIDTH)],
                        buffer.at[which % 2, operand, pl.ds(at * rows, rows)],
                        sems.at[which % 2, operand],
                    ).start()

    @pl.when(pairs[A, step] >= 0)
    def _():
        slot = step % 2
        for operand in range(2):
            here = buffer.at[slot, operand]
            pltpu.make_async_copy(here, here, sems.at[slot, operand]).wait()
        begins = pairs[BEGINS, step] != 0
        add_product(buffer.at[slot, 0], buffer.at[slot, 1], w_ref, scaled, total, begins)

    @pl.when((pairs[A, step] >= 0) & (pairs[ENDS, step] != 0))
    def _():
        terms = folded_total(total, fold_ref).reshape(out_ref.shape)
        out_ref[...] = so_far_ref[...] + terms


def list_terms(pairs, views, weights, fold, so_far):
    arrays = []
    places = []
    for parts in views:
        place = []
        for array, row in parts:
            known = [at for at, other in enumerate(arrays) if other is array]
            place.append((known[0] if known else len(arrays), row))
            if not known:
                arrays.append(array)
        places.append(place)
    _, owners, rows, _ = so_far.shape
    depth = weights.shape[0]
    block = pl.BlockSpec((1, owners, rows, NOCC), lambda g, s: (s[SLOT, g], 0, 0, 0))
    return pl.pallas_call(
        functools.partial(list_kernel, places),
        grid_spec=pltpu.PrefetchScalarGridSpec(
            num_scalar_prefetch=1,
            grid=(pairs.shape[1],),
            in_specs=[pl.BlockSpec(memory_space=pl.ANY)] * len(arrays)
            + [
                pl.BlockSpec(memory_space=pltpu.VMEM),
                pl.BlockSpec(memory_space=pltpu.VMEM),
                block,
            ],
            out_specs=block,
            scratch_shapes=[
                pltpu.VMEM((2, 2, 2 * depth, WIDTH), jnp.bfloat16),
                pltpu.VMEM((depth, 4 * WIDTH), jnp.bfloat16),
                pltpu.VMEM((WIDTH, 4 * WIDTH), jnp.float32),
                pltpu.SemaphoreType.DMA((2, 2)),
            ],
        ),
        out_shape=jax.ShapeDtypeStruct(so_far.shape, jnp.float32),
        input_output_aliases={len(arrays) + 3: 0},
        compiler_params=pltpu.CompilerParams(vmem_limit_bytes=32 * 2**20),
        cost_estimate=pl.CostEstimate(flops=0, bytes_accessed=0, transcendentals=0),
        name="list_terms",
    )(pairs, *arrays, weights, fold, so_far)


def cut_kernel(groups, me_ref, x_ref, *refs):
    *out_refs, sems = refs
    columns = x_ref.shape[1] // WIDTH
    copies = []
    for pieces, out_ref in zip(groups, out_refs):
        row = 0
        for shift, begin, rows in pieces:
            column = pl.multiple_of(lax.rem(me_ref[0] + shift, columns) * WIDTH, WIDTH)
            source = x_ref.at[pl.ds(begin, rows), pl.ds(column, out_ref.shape[1])]
            target = out_ref.at[pl.ds(row, rows)]
            copies.append(pltpu.make_async_copy(source, target, sems.at[len(copies)]))
            row += rows
    for copy in copies:
        copy.start()
    for copy in copies:
        copy.wait()


def cut(x, me, *groups, blocks=1):
    shapes = [(sum(rows for _, _, rows in pieces), blocks * WIDTH) for pieces in groups]
    count = sum(len(pieces) for pieces in groups)
    return pl.pallas_call(
        functools.partial(cut_kernel, groups),
        grid_spec=pltpu.PrefetchScalarGridSpec(
            num_scalar_prefetch=1,
            grid=(1,),
            in_specs=[pl.BlockSpec(memory_space=pl.ANY)],
            out_specs=[pl.BlockSpec(memory_space=pltpu.VMEM)] * len(shapes),
            scratch_shapes=[pltpu.SemaphoreType.DMA((count,))],
        ),
        out_shape=[jax.ShapeDtypeStruct(shape, x.dtype) for shape in shapes],
        compiler_params=pltpu.CompilerParams(vmem_limit_bytes=32 * 2**20),
        cost_estimate=pl.CostEstimate(flops=0, bytes_accessed=0, transcendentals=0),
        name="cut",
    )(me.reshape(1), x)


def weights_of(coefficients, omega):
    kernel = jnp.dot(
        coefficients, omega, precision=lax.Precision.HIGHEST, preferred_element_type=jnp.float32
    ) / math.sqrt(NAUX * NCABS)
    return kernel.T


def reduced(terms):
    owners, copies = lax.axis_size("band"), lax.axis_size("fit")
    rows = terms.shape[1]
    sent = jnp.broadcast_to(terms[:, None], (owners, copies, rows, NOCC))
    sent = sent.reshape(owners * copies, rows, NOCC)
    return lax.all_to_all(sent, ("band", "fit"), 0, 0, tiled=True).sum(0)


def neighbours(distance, x, coefficients, omega):
    owners = lax.axis_size("band")
    rows = 4 * NOCC // owners
    fold = fold_matrix(owners)
    weights = weights_of(coefficients, omega)
    height = x.shape[0]
    half = x.shape[1] // WIDTH // 2
    upward = distance == 1
    start = jnp.zeros((), jnp.int32)
    pieces = []
    at = 0
    for size in (half - half // 4, half // 4):
        low, high = [(at, 0, height)], [(half + at, 0, height)]
        up, down = cut(x, start, low, high, blocks=size)
        views = [[(shifted(up, "ka", 1), 0)], [(shifted(down, "ka", -1), 0)], [(x, 0)]]
        pieces.append((at, size, views))
        at += size

    def table(at, size, foreign):
        def columns(came, first):
            result = np.zeros((7, size), np.int32)
            place, column = (A, A_COLUMN) if foreign else (B, B_COLUMN)
            result[place], result[column] = came, np.arange(size)
            place, column = (B, B_COLUMN) if foreign else (A, A_COLUMN)
            result[place], result[column] = 2, first + np.arange(size)
            result[SLOT], result[BEGINS, 0], result[ENDS, -1] = int(foreign), 1, 1
            return result

        up, down = columns(0, at), columns(1, half + at)
        return jnp.where(upward, *((up, down) if foreign else (down, up)))

    terms = jnp.zeros((2, owners, rows, NOCC), jnp.float32)
    for at, size, views in pieces:
        pairs = jnp.concatenate([table(at, size, True), table(at, size, False)], axis=1)
        terms = list_terms(pairs, views, weights, fold, terms)
    own, foreign = terms[0], terms[1]
    own += shifted(jnp.where(upward, foreign, 0.0), "ka", -1)
    own += shifted(jnp.where(upward, 0.0, foreign), "ka", 1)
    return reduced(own)


def listed_pairs(cycle, distance):
    far = cycle // 2
    groups = [[], [], []]
    for d in range(cycle):
        blocks = (d, (d + distance) % cycle)
        late = 2 if far in blocks else int(2 in blocks or cycle - 2 in blocks)
        groups[late].append((*blocks, d))
    steps = []
    for group, length in zip(groups, (4, 4, 2)):
        idle = (-1, -1, group[-1][2])
        steps += group + [idle] * (length - len(group))
    return np.array(steps, np.int32).T


def spread(distance, x, coefficients, omega):
    owners = lax.axis_size("band")
    rows = 4 * NOCC // owners
    fold = fold_matrix(owners)
    weights = weights_of(coefficients, omega)
    cycle = lax.axis_size("ka")
    me = lax.axis_index("ka")
    size = x.shape[0]
    part = size // 2

    def whole(d):
        return (d % cycle, 0, size)

    up_long, down_long = cut(
        x, me, [whole(3), (4, 0, part)], [whole(-3), (4, part, part)]
    )
    up_short, down_short = cut(x, me, [whole(2), whole(1)], [whole(-2), whole(-1)])
    own = cut(x, me, [whole(0)])[0]

    def ring(long, short, step):
        first = shifted(long, "ka", step)
        first, _ = lax.optimization_barrier((first, short))
        short = shifted(short, "ka", step)
        second = shifted(first, "ka", step)
        third = shifted(second, "ka", step)
        return short, shifted(short[:size], "ka", step), third, shifted(third[size:], "ka", step)

    up_short, up_two, up_long, up_far = ring(up_long, up_short, 1)
    down_short, down_two, down_long, down_far = ring(down_long, down_short, -1)

    listed = np.stack([listed_pairs(cycle, min(max(t, 2), cycle - 2)) for t in range(cycle)])
    listed = jnp.asarray(listed)[distance]

    def table(begin, end):
        first, second, place = listed[:, begin:end]
        one, none = jnp.ones_like(first), jnp.zeros_like(first)
        return jnp.stack([first, second, (place + me) % cycle, one, one, none, none])

    views = [[(own, 0)]] * cycle
    views[1], views[7] = [(down_short, size)], [(up_short, size)]
    views[3], views[5] = [(down_long, 0)], [(up_long, 0)]
    terms = jnp.zeros((cycle, owners, rows, NOCC), jnp.float32)
    terms = list_terms(table(0, 4), views, weights, fold, terms)
    up_two, down_two, terms = lax.optimization_barrier((up_two, down_two, terms))
    views[2], views[6] = [(down_two, 0)], [(up_two, 0)]
    terms = list_terms(table(4, 8), views, weights, fold, terms)
    up_far, down_far, terms = lax.optimization_barrier((up_far, down_far, terms))
    views[4] = [(up_far, 0), (down_far, 0)]
    terms = list_terms(table(8, 10), views, weights, fold, terms)
    sent = terms.reshape(cycle * owners, rows, NOCC)
    mine = lax.all_to_all(sent, ("ka", "band"), 0, 0, tiled=True).sum(0)
    return lax.all_gather(mine, "fit").sum(0)


def shards(fitted, omega, coefficients, partner):
    cycle = lax.axis_size("ka")
    distance = partner[0]
    away = (distance != 1) & (distance != cycle - 1)
    x = fitted.reshape(2 * fitted.shape[2], fitted.shape[3])
    total = lax.cond(away, spread, neighbours, distance, x, coefficients, omega)
    total = total.reshape(2, 2, 1, -1, NOCC)
    return (total[0], total[1])


def solution(mesh):
    placed = (P("ka", None, "fit", "band"), P(None, "fit"), P(), P())
    return jax.shard_map(
        shards,
        mesh=mesh,
        in_specs=placed,
        out_specs=(P(None, "ka", "band", None), P(None, "ka", "band", None)),
        check_vma=False,
    )
```
